512 devices in a mesh: dp: 32 (over y_lo, z), tensor: 16 (over y_hi, x, core).
Axes of the slice: x: 4, y: 4 (y_hi: 2, y_lo: 2; y = y_hi * 2 + y_lo), z: 16, core: 2. Of those that a mesh axis runs over, the one named last changes fastest.
Arguments:
- grad: bfloat16 [8192, 14336], P('dp', 'tensor'), may hold values from -6 to 6
- left_basis: bfloat16 [8192, 1024], P('dp', 'tensor'), may hold values from -0.0625 to 0.0625
- right_basis: float32 [14336, 896], P('tensor'), may hold values from -0.1875 to 0.1875
- moments: float32 [1024, 14336], P('dp', 'tensor'), may hold values from 0.05 to 2
Outputs:
- new_moments: float32 [1024, 14336], P('dp', 'tensor')
- update: bfloat16 [8192, 14336], P('dp', 'tensor')
The draws below stay inside these ranges and needn't reach their ends.
All inputs are finite; a program needn't handle non-finite values.
Results may differ from the reference program's by a relative error of at most 0.0065.
Values may be sent and summed in bfloat16 or wider, within the bound.
A program may use at most 64 MiB of HBM per device.

```python
import math
import jax
import jax.numpy as jnp
from jax import lax

D = 8192
FF = 14336
K = 1024
CF = 896


def block_scale(key, dims, split, low, high):
    gain, own = 1.0, jax.random.fold_in(key, 6)
    for position, parts in split:
        steps = jnp.exp(jax.random.uniform(jax.random.fold_in(own, position), (parts,), jnp.float32, low / len(split), high / len(split)))
        gain = gain * jnp.repeat(steps, dims[position] // parts).reshape([-1 if axis == position else 1 for axis in range(len(dims))])
    return gain


def bell_draw(rng, dims, width, reach, shards=(), dtype=jnp.bfloat16):
    drawn = width * jax.random.normal(rng, dims, jnp.float32)
    if shards:
        drawn = drawn * block_scale(rng, dims, shards, -0.22, 0.18)
    return jnp.clip(drawn, -reach, reach).astype(dtype)


def setup_inputs(seed: int = 0) -> dict:
    arg_keys = jax.random.split(jax.random.key(seed), 5)
    return {
        "grad": bell_draw(arg_keys[0], (D, FF), 1.0, 6.0, ((0, 32), (1, 16))),
        "left_basis": bell_draw(arg_keys[1], (D, K), D ** -0.5, 0.0625, ((0, 32), (1, 16))),
        "right_basis": bell_draw(arg_keys[2], (FF, CF), CF ** -0.5, 0.1875, ((0, 16),), jnp.float32),
        "moments": jnp.clip(jnp.exp(math.log(2.0) - 3.6888794 * jax.random.uniform(arg_keys[3], (K, FF), jnp.float32) ** block_scale(arg_keys[3], (K, FF), ((0, 32), (1, 16)), -0.2, 0.2)), 0.05, 2.0),
    }


second_decay = 0.95
moment_eps = 1e-08

def reference(grad, left_basis, right_basis, moments):
    n_blocks = FF // CF
    projected = lax.dot_general(left_basis, grad, (((0,), (0,)), ((), ())), preferred_element_type=jnp.float32)
    blocks_right = right_basis.reshape(n_blocks, CF, CF)
    rotated = jnp.einsum('kbc,bcd->kbd', projected.reshape(K, n_blocks, CF), blocks_right, precision=lax.Precision.HIGHEST).reshape(K, FF)
    new_moments = second_decay * moments + (1.0 - second_decay) * rotated * rotated
    scaled = (rotated / jnp.sqrt(new_moments + moment_eps)).astype(jnp.bfloat16)
    unrotated = jnp.einsum('kbd,bcd->kbc', scaled.astype(jnp.float32).reshape(K, n_blocks, CF), blocks_right, precision=lax.Precision.HIGHEST)
    unrotated = unrotated.reshape(K, FF).astype(jnp.bfloat16)
    update = jnp.dot(left_basis, unrotated, preferred_element_type=jnp.float32).astype(jnp.bfloat16)
    return (new_moments, update)
```

```python
import jax
import jax.numpy as jnp
from jax import lax
from jax.sharding import PartitionSpec as P

second_decay = 0.95
moment_eps = 1e-08


def right_apply(values, right_block):
    return jnp.dot(values, right_block, precision=lax.Precision.HIGHEST)


def right_undo(values, right_block):
    return lax.dot_general(
        values, right_block, (((1,), (1,)), ((), ())), precision=lax.Precision.HIGHEST
    )


def rescale(rotated, moments):
    new_moments = second_decay * moments + (1.0 - second_decay) * rotated * rotated
    scaled = (rotated / jnp.sqrt(new_moments + moment_eps)).astype(jnp.bfloat16)
    return (new_moments, scaled)


def per_device(grad, left_basis, right_basis, moments):
    left_rows = lax.all_gather(left_basis, "tensor", axis=1, tiled=True)
    projected = lax.psum_scatter(
        lax.dot_general(
            left_rows, grad, (((0,), (0,)), ((), ())), preferred_element_type=jnp.float32
        ),
        "dp",
        scatter_dimension=0,
        tiled=True,
    )
    rotated = right_apply(projected, right_basis)
    new_moments, scaled = rescale(rotated, moments)
    unrotated = right_undo(scaled.astype(jnp.float32), right_basis).astype(jnp.bfloat16)
    gathered = lax.all_gather(unrotated, "dp", axis=0, tiled=True)
    accumulated = jnp.dot(left_rows, gathered, preferred_element_type=jnp.float32)
    return (new_moments, accumulated.astype(jnp.bfloat16))


def solution(mesh):
    return jax.shard_map(
        per_device,
        mesh=mesh,
        in_specs=(P("dp", "tensor"), P("dp", "tensor"), P("tensor", None), P("dp", "tensor")),
        out_specs=(P("dp", "tensor"), P("dp", "tensor")),
        check_vma=False,
    )
```

```python
import functools

import jax
import jax.numpy as jnp
from jax import lax
from jax.experimental import pallas as pl
from jax.experimental.pallas import tpu as pltpu
from jax.sharding import PartitionSpec as P

second_decay = 0.95
moment_eps = 1e-08

MESH = pl.DeviceIdType.MESH
Z, X = 16, 4
ROWS, COLS, OWN, SHARD = 256, 896, 32, 64
HALF = Z * OWN
JS = 2 * X
SPANS = ((0, 256), (256, 256), (512, 384))
NC = len(SPANS)
HOPS = tuple((8, 7) if c % 2 == 0 else (7, 8) for c in range(NC))


def split_bf16(values):
    high = values.astype(jnp.bfloat16)
    return high, (values - high.astype(jnp.float32)).astype(jnp.bfloat16)


def dot(a, b, ca, cb):
    return lax.dot_general(a, b, (((ca,), (cb,)), ((), ())), preferred_element_type=jnp.float32)


def kernel(grad, left, right, moments, new_moments, update, *scratch):
    (mine, shards, other, lrow, rows, w32, whi, wlo, mom, proj, rot) = scratch[:11]
    first, slots, gathered = (scratch[11 + NC * i : 11 + NC * (i + 1)] for i in range(3))
    (loc_s, l1_s, l1_r, lx_s, lx_r, lc_s, lc_r, g_s, g_r, o_s, o_r, rs_s, rs_r, y_s, y_r, ag_s, ag_r) = scratch[
        11 + 3 * NC :
    ]
    dp, t = lax.axis_index("dp"), lax.axis_index("tensor")
    ylo, z = dp // Z, dp % Z
    yhi, j = t // JS, t % JS
    x, core = j // 2, j % 2
    plane = ylo * Z
    up = (plane + (z + 1) % Z, t)
    down = (plane + (z + Z - 1) % Z, t)
    partner = ((1 - ylo) * Z + z, t)
    across = (dp, (1 - yhi) * JS + j)
    diagonal = ((1 - ylo) * Z + z, (1 - yhi) * JS + j)
    sibling = (dp, yhi * JS + x * 2 + (1 - core))
    xs = [(dp, yhi * JS + ((x + d) % X) * 2 + core) for d in range(1, X)]

    def remote(src, dst, ssem, rsem, dev):
        return pltpu.make_async_remote_copy(
            src_ref=src, dst_ref=dst, send_sem=ssem, recv_sem=rsem, device_id=dev, device_id_type=MESH
        )

    barrier = pltpu.get_barrier_semaphore()
    everyone = [up, down, partner, across, diagonal, sibling] + xs
    for dev in everyone:
        pl.semaphore_signal(barrier, inc=1, device_id=dev, device_id_type=MESH)
    loads = [
        pltpu.make_async_copy(grad, rows.at[ylo], loc_s.at[0]),
        pltpu.make_async_copy(right, w32, loc_s.at[1]),
        pltpu.make_async_copy(moments, mom, loc_s.at[2]),
    ]
    for load in loads:
        load.start()
    mine[...] = left[...].T
    pl.semaphore_wait(barrier, len(everyone))

    at_home = ylo == yhi
    here = shards.at[ylo, j]

    @pl.when(at_home)
    def _():
        remote(mine, here, l1_s.at[0], l1_r.at[ylo], across).start()
        shards[ylo, j] = mine[...]

    @pl.when(jnp.logical_not(at_home))
    def _():
        remote(mine, here, l1_s.at[0], l1_r.at[ylo], partner).start()
        remote(mine, here, l1_s.at[1], l1_r.at[ylo], diagonal).start()

    def grad_part(c):
        lo, n = SPANS[c]
        return remote(
            grad.at[:, pl.ds(lo, n)], rows.at[ylo, :, pl.ds(lo, n)], g_s.at[c], g_r.at[c], partner
        )

    for c in range(NC):
        grad_part(c).start()

    def to_x(r, d):
        return remote(shards.at[r, j], shards.at[r, j], lx_s.at[r, d], lx_r.at[r, d], xs[d])

    def from_x(r, d):
        jj = ((x + X - 1 - d) % X) * 2 + core
        return remote(shards.at[r, jj], shards.at[r, jj], lx_s.at[r, d], lx_r.at[r, d], xs[d])

    def to_core(r, d):
        jj = ((x + X - d) % X) * 2 + core
        return remote(shards.at[r, jj], shards.at[r, jj], lc_s.at[r, d], lc_r.at[r, d], sibling)

    def from_core(r, d):
        jj = ((x + X - d) % X) * 2 + (1 - core)
        return remote(shards.at[r, jj], shards.at[r, jj], lc_s.at[r, d], lc_r.at[r, d], sibling)

    for r in range(2):

        @pl.when(jnp.logical_not(jnp.logical_and(at_home, ylo == r)))
        def _():
            remote(mine, shards.at[r, j], l1_s.at[0], l1_r.at[r], across).wait_recv()

        for d in range(X - 1):
            to_x(r, d).start()
        to_core(r, 0).start()

    loads[1].wait()
    for lo in range(0, COLS, 128):
        high, low = split_bf16(w32[pl.ds(lo, 128), :])
        whi[pl.ds(lo, 128), :] = high
        wlo[pl.ds(lo, 128), :] = low

    for r in range(2):
        for d in range(X - 1):
            from_x(r, d).wait_recv()
            to_core(r, d + 1).start()
    for r in range(2):
        for d in range(X):
            from_core(r, d).wait_recv()
    loads[0].wait()

    def rs(c, way, s):
        hops = HOPS[c]
        src = first[c].at[way] if s == 0 else slots[c].at[way, s - 1]
        return remote(src, slots[c].at[way, s], rs_s.at[c, way, s], rs_r.at[c, way, s], (up, down)[way])

    def part(c, d):
        lo, n = SPANS[c]
        return proj[pl.ds(pl.multiple_of(d * OWN, OWN), OWN), pl.ds(lo, n)]

    def bound_for(c, way, s):
        return (z + HOPS[c][0] - s) % Z if way == 0 else (z + Z - HOPS[c][1] + s) % Z

    for c, (lo, n) in enumerate(SPANS):
        grad_part(c).wait_recv()
        total = dot(shards[0].reshape(HALF, ROWS), rows[0, :, pl.ds(lo, n)], 1, 0)
        total += dot(shards[1].reshape(HALF, ROWS), rows[1, :, pl.ds(lo, n)], 1, 0)
        proj[:, pl.ds(lo, n)] = total
        for way in range(2):
            first[c][way] = part(c, bound_for(c, way, 0)).astype(jnp.bfloat16)
            rs(c, way, 0).start()

    def to_partner():
        return remote(shards.at[1 - ylo], other, o_s, o_r, partner)

    to_partner().start()
    for s in range(1, 8):
        for c in range(NC):
            for way in range(2):
                if s < HOPS[c][way]:
                    rs(c, way, s - 1).wait_recv()
                    held = slots[c].at[way, s - 1]
                    held[...] = (held[...].astype(jnp.float32) + part(c, bound_for(c, way, s))).astype(jnp.bfloat16)
                    rs(c, way, s).start()
        if s == 2:
            lrow[ylo] = shards[ylo].reshape(HALF, ROWS).T
        if s == 5:
            to_partner().wait_recv()
            lrow[1 - ylo] = other[...].reshape(HALF, ROWS).T

    loads[2].wait()
    for c, (lo, n) in enumerate(SPANS):
        own = part(c, z)
        for way in range(2):
            last = HOPS[c][way] - 1
            rs(c, way, last).wait_recv()
            own += slots[c][way, last].astype(jnp.float32)
        high, low = split_bf16(own)
        both = dot(jnp.concatenate([high, low], axis=0), whi[pl.ds(lo, n), :], 1, 0)
        term = both[:OWN] + both[OWN:] + dot(high, wlo[pl.ds(lo, n), :], 1, 0)
        if c == 0:
            rot[...] = term
        else:
            rot[...] += term
    rotated = rot[...]
    moved = second_decay * mom[...] + (1.0 - second_decay) * rotated * rotated
    new_moments[...] = moved
    scaled = (rotated / jnp.sqrt(moved + moment_eps)).astype(jnp.bfloat16)

    def y_part(c):
        ref = gathered[c].at[ylo, z]
        return remote(ref, ref, y_s.at[c], y_r.at[c], partner)

    def ag(c, way, s):
        o = (z + Z - s) % Z if way == 0 else (z + s) % Z
        ref = gathered[c].at[:, o]
        return remote(ref, ref, ag_s.at[c, way, s], ag_r.at[c, way, s], (up, down)[way])

    def ag_in(c, way, s):
        o = (z + Z - 1 - s) % Z if way == 0 else (z + 1 + s) % Z
        ref = gathered[c].at[:, o]
        return remote(ref, ref, ag_s.at[c, way, s], ag_r.at[c, way, s], (up, down)[way])

    for c, (lo, n) in enumerate(SPANS):
        back = dot(scaled, whi[pl.ds(lo, n), :], 1, 1) + dot(scaled, wlo[pl.ds(lo, n), :], 1, 1)
        gathered[c][ylo, z] = back.astype(jnp.bfloat16)
        y_part(c).start()
    for c in range(NC):
        ref = gathered[c].at[1 - ylo, z]
        remote(ref, ref, y_s.at[c], y_r.at[c], partner).wait_recv()
        for way in range(2):
            ag(c, way, 0).start()
    for s in range(1, 8):
        for c in range(NC):
            for way in range(2):
                if s < HOPS[c][way]:
                    ag_in(c, way, s - 1).wait_recv()
                    ag(c, way, s).start()
    for c, (lo, n) in enumerate(SPANS):
        for way in range(2):
            ag_in(c, way, HOPS[c][way] - 1).wait_recv()
        total = dot(lrow[0], gathered[c][0].reshape(HALF, n), 1, 0)
        total += dot(lrow[1], gathered[c][1].reshape(HALF, n), 1, 0)
        update[:, pl.ds(lo, n)] = total.astype(jnp.bfloat16)

    remote(mine, here, l1_s.at[0], l1_r.at[0], across).wait_send()

    @pl.when(jnp.logical_not(at_home))
    def _():
        remote(mine, here, l1_s.at[1], l1_r.at[0], diagonal).wait_send()

    for r in range(2):
        for d in range(X - 1):
            to_x(r, d).wait_send()
        for d in range(X):
            to_core(r, d).wait_send()
    to_partner().wait_send()
    for c in range(NC):
        grad_part(c).wait_send()
        y_part(c).wait_send()
        for way in range(2):
            for s in range(HOPS[c][way]):
                rs(c, way, s).wait_send()
                ag(c, way, s).wait_send()


def per_device(grad, left_basis, right_basis, moments):
    bf16, f32 = jnp.bfloat16, jnp.float32
    dma = pltpu.SemaphoreType.DMA
    vmem = pl.BlockSpec(memory_space=pltpu.VMEM)
    hbm = pl.BlockSpec(memory_space=pl.ANY)
    scratch = [
        pltpu.VMEM((SHARD, ROWS), bf16),
        pltpu.VMEM((2, JS, SHARD, ROWS), bf16),
        pltpu.VMEM((JS, SHARD, ROWS), bf16),
        pltpu.VMEM((2, ROWS, HALF), bf16),
        pltpu.VMEM((2, ROWS, COLS), bf16),
        pltpu.VMEM((COLS, COLS), f32),
        pltpu.VMEM((COLS, COLS), bf16),
        pltpu.VMEM((COLS, COLS), bf16),
        pltpu.VMEM((OWN, COLS), f32),
        pltpu.VMEM((HALF, COLS), f32),
        pltpu.VMEM((OWN, COLS), f32),
    ]
    scratch += [pltpu.VMEM((2, OWN, n), bf16) for _, n in SPANS]
    scratch += [pltpu.VMEM((2, 8, OWN, n), bf16) for _, n in SPANS]
    scratch += [pltpu.VMEM((2, Z, OWN, n), bf16) for _, n in SPANS]
    scratch += [dma((3,)), dma((2,)), dma((2,)), dma((2, 3)), dma((2, 3)), dma((2, 4)), dma((2, 4))]
    scratch += [dma((NC,)), dma((NC,)), dma, dma, dma((NC, 2, 8)), dma((NC, 2, 8))]
    scratch += [dma((NC,)), dma((NC,)), dma((NC, 2, 8)), dma((NC, 2, 8))]
    return pl.pallas_call(
        kernel,
        out_shape=(
            jax.ShapeDtypeStruct((OWN, COLS), f32),
            jax.ShapeDtypeStruct((ROWS, COLS), bf16),
        ),
        in_specs=[hbm, vmem, hbm, hbm],
        out_specs=(vmem, vmem),
        scratch_shapes=scratch,
        compiler_params=pltpu.CompilerParams(
            collective_id=0, has_side_effects=True, vmem_limit_bytes=48 * 2**20
        ),
    )(grad, left_basis, right_basis, moments)


def solution(mesh):
    return jax.shard_map(
        per_device,
        mesh=mesh,
        in_specs=(P("dp", "tensor"), P("dp", "tensor"), P("tensor", None), P("dp", "tensor")),
        out_specs=(P("dp", "tensor"), P("dp", "tensor")),
        check_vma=False,
    )
```

```python
import jax
import jax.numpy as jnp
from jax import lax
from jax.experimental import pallas as pl
from jax.experimental.pallas import tpu as pltpu
from jax.sharding import PartitionSpec as P

second_decay = 0.95
moment_eps = 1e-08

MESH = pl.DeviceIdType.MESH
Z, X = 16, 4
ROWS, COLS, OWN, SHARD = 256, 896, 32, 64
HALF = Z * OWN
JS = 2 * X
SPANS = ((0, 256), (256, 256), (512, 256), (768, 128))
PART = OWN // 2
GPARTS = 4


def split_bf16(values):
    high = values.astype(jnp.bfloat16)
    return high, (values - high.astype(jnp.float32)).astype(jnp.bfloat16)


def dot(a, b, ca, cb):
    return lax.dot_general(a, b, (((ca,), (cb,)), ((), ())), preferred_element_type=jnp.float32)


def kernel(grad, left, right, moments, new_moments, update, *scratch):
    (shards, other, lrow, rows, w32, whi, wlo, mom, proj, leaving, slots, gathered, total) = scratch[:13]
    (loc_s, l_s, l_r, lx_s, lx_r, lc_s, lc_r, g_s, g_r, o_s, o_r, rs_s, rc_r, rl_r, ag_s, ac_r, al_r, y_s, y_r) = (
        scratch[13:]
    )
    dp, t = lax.axis_index("dp"), lax.axis_index("tensor")
    ylo, z = dp // Z, dp % Z
    yhi, j = t // JS, t % JS
    x, core = j // 2, j % 2

    def along(step):
        return (ylo * Z + (z + Z + step) % Z, t)

    near, far = (along(1), along(-1)), (along(2), along(-2))
    partner = ((1 - ylo) * Z + z, t)
    across = (dp, (1 - yhi) * JS + j)
    diagonal = ((1 - ylo) * Z + z, (1 - yhi) * JS + j)
    sibling = (dp, yhi * JS + x * 2 + (1 - core))
    xs = [(dp, yhi * JS + ((x + d) % X) * 2 + core) for d in range(1, X)]

    def remote(src, dst, ssem, rsem, dev):
        return pltpu.make_async_remote_copy(
            src_ref=src, dst_ref=dst, send_sem=ssem, recv_sem=rsem, device_id=dev, device_id_type=MESH
        )

    barrier = pltpu.get_barrier_semaphore()
    everyone = [*near, *far, partner, across, diagonal, sibling] + xs
    for dev in everyone:
        pl.semaphore_signal(barrier, inc=1, device_id=dev, device_id_type=MESH)
    here = shards.at[ylo, core, x]
    loads = [
        pltpu.make_async_copy(grad, rows.at[ylo], loc_s.at[0]),
        pltpu.make_async_copy(right, w32, loc_s.at[1]),
        pltpu.make_async_copy(moments, mom, loc_s.at[2]),
    ]
    keep = pltpu.make_async_copy(left, here, loc_s.at[3])
    at_home = ylo == yhi
    away = jnp.logical_not(at_home)
    pl.when(at_home)(keep.start)
    for load in loads:
        load.start()
    pl.semaphore_wait(barrier, len(everyone))

    to_across = remote(left, here, l_s.at[0], l_r.at[ylo], across)
    to_mate = remote(left, here, l_s.at[0], l_r.at[ylo], partner)
    to_diagonal = remote(left, here, l_s.at[1], l_r.at[ylo], diagonal)
    pl.when(at_home)(to_across.start)
    pl.when(away)(to_mate.start)
    pl.when(away)(to_diagonal.start)

    def grad_part(p):
        cut = pl.ds(p * (ROWS // GPARTS), ROWS // GPARTS)
        return remote(grad.at[cut], rows.at[ylo, cut], g_s, g_r, partner)

    for p in range(GPARTS):
        grad_part(p).start()

    def to_x(r, d):
        ref = shards.at[r, core, x]
        return remote(ref, ref, lx_s.at[r, d - 1], lx_r.at[r, d - 1], xs[d - 1])

    def from_x(r, d):
        ref = shards.at[r, core, (x + X - d) % X]
        return remote(ref, ref, lx_s.at[r, d - 1], lx_r.at[r, d - 1], xs[d - 1])

    def to_core(r):
        ref = shards.at[r, core]
        return remote(ref, ref, lc_s.at[r], lc_r.at[r], sibling)

    def from_core(r):
        ref = shards.at[r, 1 - core]
        return remote(ref, ref, lc_s.at[r], lc_r.at[r], sibling)

    for k in range(2):
        r = (ylo + k) % 2
        arrived = remote(left, shards.at[r, core, x], l_s.at[0], l_r.at[r], sibling).wait_recv
        if k == 0:
            pl.when(at_home)(keep.wait)
            pl.when(away)(arrived)
        else:
            arrived()
        for d in range(1, X):
            to_x(r, d).start()

    loads[1].wait()
    for lo in range(0, COLS, 128):
        high, low = split_bf16(w32[pl.ds(lo, 128), :])
        whi[pl.ds(lo, 128), :] = high
        wlo[pl.ds(lo, 128), :] = low

    for k in range(2):
        r = (ylo + k) % 2
        for d in range(1, X):
            from_x(r, d).wait_recv()
        to_core(r).start()

    def project(c):
        for lo, n in SPANS:
            part = dot(shards[0, c].reshape(X * SHARD, ROWS), rows[0, :, pl.ds(lo, n)], 1, 0)
            part += dot(shards[1, c].reshape(X * SHARD, ROWS), rows[1, :, pl.ds(lo, n)], 1, 0)
            proj[pl.ds(pl.multiple_of(c * X * SHARD, X * SHARD), X * SHARD), pl.ds(lo, n)] = part

    loads[0].wait()
    remote(grad, rows.at[1 - ylo], g_s, g_r, partner).wait_recv()
    project(core)
    for r in range(2):
        from_core(r).wait_recv()
    project(1 - core)

    def chunk(d, p=None):
        d = (d + Z) % Z
        row = ((d // 2) % 2) * (X * SHARD) + (d // 4) * SHARD + (d % 2) * OWN
        if p is None:
            return proj[pl.ds(pl.multiple_of(row, OWN), OWN), :]
        return proj[pl.ds(pl.multiple_of(row + p * PART, PART), PART), :]

    def half(ref, p):
        return ref.at[pl.ds(p * PART, PART)]

    def chain_in(way, k):
        return slots.at[4 * way + k]

    def leaf_in(way, k):
        return slots.at[7 + 4 * way + k]

    def chain_source(way, k):
        if way == 0:
            return leaving.at[0] if k == 0 else chain_in(0, k - 1)
        return leaf_in(1, k)

    def rs_chain(way, k, p):
        return remote(
            half(chain_source(way, k), p), half(chain_in(way, k), p), rs_s, rc_r.at[way, k, p], far[way]
        )

    def rs_leaf(way, k):
        return remote(leaving.at[1 + 4 * way + k], leaf_in(way, k), rs_s, rl_r.at[way, k], near[way])

    def send_leaf(way, k):
        leaving[1 + 4 * way + k] = chunk(z + 7 - 2 * k if way == 0 else z - 7 + 2 * k).astype(jnp.bfloat16)
        rs_leaf(way, k).start()

    def send_chain(way, k):
        first = way == 0 and k == 0
        if not first:
            rs_leaf(way, k - 1 if way == 0 else k).wait_recv()
        for p in range(2):
            mine = chunk(z + 8 - 2 * k if way == 0 else z - 6 + 2 * k, p)
            if not first:
                leaf = leaf_in(way, k - 1 if way == 0 else k)
                mine += half(leaf, p)[...].astype(jnp.float32)
            if k > 0:
                rs_chain(way, k - 1, p).wait_recv()
                mine += half(chain_in(way, k - 1), p)[...].astype(jnp.float32)
            half(chain_source(way, k), p)[...] = mine.astype(jnp.bfloat16)
            rs_chain(way, k, p).start()

    def to_partner():
        return remote(shards.at[1 - ylo], other, o_s, o_r, partner)

    def turn(h, ref, xx):
        piece = jnp.concatenate([ref[0, xx], ref[1, xx]], axis=0)
        lrow[h, :, pl.ds(xx * 2 * SHARD, 2 * SHARD)] = piece.T

    send_chain(0, 0)
    send_leaf(1, 0)
    send_leaf(0, 0)
    send_leaf(1, 1)
    to_partner().start()
    turn(ylo, shards.at[ylo], 0)
    for k in range(3):
        send_chain(1, k)
        send_chain(0, k + 1)
        send_leaf(0, k + 1)
        if k < 2:
            send_leaf(1, k + 2)
        turn(ylo, shards.at[ylo], k + 1)

    loads[2].wait()
    own = chunk(z)
    for way in range(2):
        rs_leaf(way, 3).wait_recv()
        own += leaf_in(way, 3)[...].astype(jnp.float32)
    for way in (1, 0):
        for p in range(2):
            rs_chain(way, 3 - way, p).wait_recv()
        own += chain_in(way, 3 - way)[...].astype(jnp.float32)
    high, low = split_bf16(own)
    both = dot(jnp.concatenate([high, low], axis=0), whi[...], 1, 0)
    rotated = both[:OWN] + both[OWN:] + dot(high, wlo[...], 1, 0)
    moved = second_decay * mom[...] + (1.0 - second_decay) * rotated * rotated
    new_moments[...] = moved
    scaled = (rotated / jnp.sqrt(moved + moment_eps)).astype(jnp.bfloat16)
    back = dot(scaled, whi[...], 1, 1) + dot(scaled, wlo[...], 1, 1)
    gathered[ylo, z] = back.astype(jnp.bfloat16)

    def origin(way, o):
        return gathered.at[ylo, (z + Z - o) % Z if way == 0 else (z + o) % Z]

    def ag_chain(way, k, p, back=0):
        ref = half(origin(way, 2 * k + back), p)
        return remote(ref, ref, ag_s, ac_r.at[way, k, p], far[way])

    def ag_leaf(way, k, back=0):
        ref = origin(way, 2 * k + back)
        return remote(ref, ref, ag_s, al_r.at[way, k], near[way])

    def forward(way, o):
        ref = origin(way, o)
        remote(ref, ref, y_s, y_r, partner).start()

    for k in range(5):
        for way in range(2):
            last = 3 - way
            if k <= last + 1:
                for p in range(2):
                    if k > 0:
                        ag_chain(way, k - 1, p, 2).wait_recv()
                    if k <= last:
                        ag_chain(way, k, p).start()
                if k < 4:
                    ag_leaf(way, k).start()
        if k == 0:
            forward(0, 0)
        else:
            for way in range(2):
                if k <= 4 - way:
                    forward(way, 2 * k)
            for way in range(2):
                ag_leaf(way, k - 1, 1).wait_recv()
                forward(way, 2 * k - 1)
        if k == 0:
            to_partner().wait_recv()
        if k < 4:
            turn(1 - ylo, other, k)

    for lo, n in SPANS:
        total[:, pl.ds(lo, n)] = dot(lrow[ylo], gathered[ylo, :, :, pl.ds(lo, n)].reshape(HALF, n), 1, 0)
    whole = gathered.at[1 - ylo]
    remote(whole, whole, y_s, y_r, partner).wait_recv()
    for lo, n in SPANS:
        rest = dot(lrow[1 - ylo], gathered[1 - ylo, :, :, pl.ds(lo, n)].reshape(HALF, n), 1, 0)
        update[:, pl.ds(lo, n)] = (total[:, pl.ds(lo, n)] + rest).astype(jnp.bfloat16)

    pl.when(at_home)(to_across.wait_send)
    pl.when(away)(to_mate.wait_send)
    pl.when(away)(to_diagonal.wait_send)
    for r in range(2):
        for d in range(1, X):
            to_x(r, d).wait_send()
        to_core(r).wait_send()
    to_partner().wait_send()
    remote(rows.at[ylo], rows.at[ylo], g_s, g_r, partner).wait_send()
    remote(slots, slots, rs_s, o_r, partner).wait_send()
    sent = gathered.at[ylo, pl.ds(0, Z - 1)]
    remote(sent, sent, ag_s, o_r, partner).wait_send()
    remote(whole, whole, y_s, y_r, partner).wait_send()


def per_device(grad, left_basis, right_basis, moments):
    bf16, f32 = jnp.bfloat16, jnp.float32
    dma = pltpu.SemaphoreType.DMA
    vmem = pl.BlockSpec(memory_space=pltpu.VMEM)
    hbm = pl.BlockSpec(memory_space=pl.ANY)
    scratch = [
        pltpu.VMEM((2, 2, X, SHARD, ROWS), bf16),
        pltpu.VMEM((2, X, SHARD, ROWS), bf16),
        pltpu.VMEM((2, ROWS, HALF), bf16),
        pltpu.VMEM((2, ROWS, COLS), bf16),
        pltpu.VMEM((COLS, COLS), f32),
        pltpu.VMEM((COLS, COLS), bf16),
        pltpu.VMEM((COLS, COLS), bf16),
        pltpu.VMEM((OWN, COLS), f32),
        pltpu.VMEM((HALF, COLS), f32),
        pltpu.VMEM((9, OWN, COLS), bf16),
        pltpu.VMEM((15, OWN, COLS), bf16),
        pltpu.VMEM((2, Z, OWN, COLS), bf16),
        pltpu.VMEM((ROWS, COLS), f32),
    ]
    scratch += [dma((4,)), dma((2,)), dma((2,)), dma((2, 3)), dma((2, 3)), dma((2,)), dma((2,)), dma, dma, dma, dma]
    scratch += [dma, dma((2, 4, 2)), dma((2, 4)), dma, dma((2, 4, 2)), dma((2, 4)), dma, dma]
    return pl.pallas_call(
        kernel,
        out_shape=(
            jax.ShapeDtypeStruct((OWN, COLS), f32),
            jax.ShapeDtypeStruct((ROWS, COLS), bf16),
        ),
        in_specs=[hbm, hbm, hbm, hbm],
        out_specs=(vmem, vmem),
        scratch_shapes=scratch,
        compiler_params=pltpu.CompilerParams(
            collective_id=0, has_side_effects=True, vmem_limit_bytes=62 * 2**20
        ),
    )(grad, left_basis.T, right_basis, moments)


def solution(mesh):
    return jax.shard_map(
        per_device,
        mesh=mesh,
        in_specs=(P("dp", "tensor"), P("dp", "tensor"), P("tensor", None), P("dp", "tensor")),
        out_specs=(P("dp", "tensor"), P("dp", "tensor")),
        check_vma=False,
    )
```

```python
import jax
import jax.numpy as jnp
from jax import lax
from jax.experimental import pallas as pl
from jax.experimental.pallas import tpu as pltpu
from jax.sharding import PartitionSpec as P

second_decay = 0.95
moment_eps = 1e-08

MESH = pl.DeviceIdType.MESH
Z, X = 16, 4
ROWS, COLS, OWN, SHARD = 256, 896, 32, 64
HALF = Z * OWN
JS = 2 * X
SPANS = ((0, 256), (256, 256), (512, 256), (768, 128))
PART = OWN // 2
GPARTS = 4
GFIRST = 2


def split_bf16(values):
    high = values.astype(jnp.bfloat16)
    return high, (values - high.astype(jnp.float32)).astype(jnp.bfloat16)


def dot(a, b, ca, cb):
    return lax.dot_general(a, b, (((ca,), (cb,)), ((), ())), preferred_element_type=jnp.float32)


def kernel(grad, left, right, moments, new_moments, update, *scratch):
    (shards, other, lrow, rows, w32, whi, wlo, mom, proj, leaving, slots, gathered, total) = scratch[:13]
    (loc_s, l_s, l_r, lx_s, lx_r, lc_s, lc_r, g_s, g_r, o_s, o_r, od_s, od_r) = scratch[13:26]
    (rs_s, rc_r, rl_r, ag_s, ac_r, al_r, y_s, y_r) = scratch[26:]
    dp, t = lax.axis_index("dp"), lax.axis_index("tensor")
    ylo, z = dp // Z, dp % Z
    yhi, j = t // JS, t % JS
    x, core = j // 2, j % 2
    is0, is1 = core == 0, core == 1

    def along(step):
        return (ylo * Z + (z + Z + step) % Z, t)

    near, far = (along(1), along(-1)), (along(2), along(-2))
    partner = ((1 - ylo) * Z + z, t)
    across = (dp, (1 - yhi) * JS + j)
    diagonal = ((1 - ylo) * Z + z, (1 - yhi) * JS + j)
    sibling = (dp, yhi * JS + x * 2 + (1 - core))
    xs = [(dp, yhi * JS + ((x + d) % X) * 2 + core) for d in range(1, X)]

    def remote(src, dst, ssem, rsem, dev):
        return pltpu.make_async_remote_copy(
            src_ref=src, dst_ref=dst, send_sem=ssem, recv_sem=rsem, device_id=dev, device_id_type=MESH
        )

    barrier = pltpu.get_barrier_semaphore()
    everyone = [*near, *far, partner, across, diagonal, sibling] + xs
    for dev in everyone:
        pl.semaphore_signal(barrier, inc=1, device_id=dev, device_id_type=MESH)
    here = shards.at[ylo, core, x]
    loads = [
        pltpu.make_async_copy(grad, rows.at[ylo], loc_s.at[0]),
        pltpu.make_async_copy(right, w32, loc_s.at[1]),
        pltpu.make_async_copy(moments, mom, loc_s.at[2]),
    ]
    keep = pltpu.make_async_copy(left, here, loc_s.at[3])
    at_home = ylo == yhi
    away = jnp.logical_not(at_home)
    pl.when(at_home)(keep.start)
    for load in loads:
        load.start()
    pl.semaphore_wait(barrier, len(everyone))

    to_across = remote(left, here, l_s.at[0], l_r.at[ylo], across)
    to_mate = remote(left, here, l_s.at[0], l_r.at[ylo], partner)
    to_diagonal = remote(left, here, l_s.at[1], l_r.at[ylo], diagonal)
    pl.when(at_home)(to_across.start)
    pl.when(away)(to_mate.start)
    pl.when(away)(to_diagonal.start)

    def grad_part(p):
        cut = pl.ds(p * (ROWS // GPARTS), ROWS // GPARTS)
        return remote(grad.at[cut], rows.at[ylo, cut], g_s, g_r, partner)

    for p in range(GFIRST):
        grad_part(p).start()

    def to_x(r, d):
        ref = shards.at[r, core, x]
        return remote(ref, ref, lx_s.at[r, d - 1], lx_r.at[r, d - 1], xs[d - 1])

    def from_x(r, d):
        ref = shards.at[r, core, (x + X - d) % X]
        return remote(ref, ref, lx_s.at[r, d - 1], lx_r.at[r, d - 1], xs[d - 1])

    def to_core(r):
        ref = shards.at[r, core]
        return remote(ref, ref, lc_s.at[r], lc_r.at[r], sibling)

    def from_core(r):
        ref = shards.at[r, 1 - core]
        return remote(ref, ref, lc_s.at[r], lc_r.at[r], sibling)

    for k in range(2):
        r = (ylo + k) % 2
        arrived = remote(left, shards.at[r, core, x], l_s.at[0], l_r.at[r], sibling).wait_recv
        if k == 0:
            pl.when(at_home)(keep.wait)
            pl.when(away)(arrived)
        else:
            arrived()
        for d in range(1, X):
            to_x(r, d).start()

    for p in range(GFIRST, GPARTS):
        grad_part(p).start()
    loads[1].wait()
    for lo in range(0, COLS, 128):
        high, low = split_bf16(w32[pl.ds(lo, 128), :])
        whi[pl.ds(lo, 128), :] = high
        wlo[pl.ds(lo, 128), :] = low

    for k in range(2):
        r = (ylo + k) % 2
        for d in range(1, X):
            from_x(r, d).wait_recv()
        to_core(r).start()

    loads[0].wait()
    remote(grad, rows.at[1 - ylo], g_s, g_r, partner).wait_recv()
    for r in range(2):
        from_core(r).wait_recv()

    def project(p):
        for lo, n in SPANS:
            part = sum(
                dot(shards[r, :, :, :, p].reshape(HALF // 2, ROWS), rows[r, :, pl.ds(lo, n)], 1, 0) for r in range(2)
            )
            proj[p, :, :, pl.ds(lo, n)] = part.reshape(Z, PART, n)

    def chunk(d, p):
        d = (d + Z) % Z
        return proj[p, ((d // 2) % 2) * JS + (d // 4) * 2 + d % 2]

    def chain_in(way, k, p):
        return slots.at[4 * way + k, p]

    def leaf_in(way, k, p):
        return slots.at[7 + 4 * way + k, p]

    def chain_source(way, k, p):
        if way == 0:
            return leaving.at[0, p] if k == 0 else chain_in(0, k - 1, p)
        return leaf_in(1, k, p)

    def rs_chain(way, k, p):
        return remote(chain_source(way, k, p), chain_in(way, k, p), rs_s, rc_r.at[way, k, p], far[way])

    def rs_leaf(way, k, p):
        return remote(leaving.at[1 + 4 * way + k, p], leaf_in(way, k, p), rs_s, rl_r.at[way, k, p], near[way])

    def send_leaf(way, k, p):
        leaving[1 + 4 * way + k, p] = chunk(z + 7 - 2 * k if way == 0 else z - 7 + 2 * k, p).astype(jnp.bfloat16)
        rs_leaf(way, k, p).start()

    def send_chain(way, k, p):
        mine = chunk(z + 8 - 2 * k if way == 0 else z - 6 + 2 * k, p)
        leaf = k - 1 if way == 0 else k
        if leaf >= 0:
            rs_leaf(way, leaf, p).wait_recv()
            mine += leaf_in(way, leaf, p)[...].astype(jnp.float32)
        if k > 0:
            rs_chain(way, k - 1, p).wait_recv()
            mine += chain_in(way, k - 1, p)[...].astype(jnp.float32)
        chain_source(way, k, p)[...] = mine.astype(jnp.bfloat16)
        rs_chain(way, k, p).start()

    def sum_step(k, p):
        if k > 0:
            send_chain(1, k - 1, p)
        send_chain(0, k, p)
        if k == 0:
            send_leaf(1, 0, p)
        send_leaf(0, k, p)
        if k < 3:
            send_leaf(1, k + 1, p)

    def to_partner(c, xx):
        return remote(shards.at[1 - ylo, c, xx], other.at[c, xx], o_s, o_r, partner)

    def all_from_partner():
        return remote(other, other, o_s, o_r, partner)

    def across_cores():
        return remote(other, other, od_s, od_r, sibling)

    def turn(h, ref, xx):
        piece = jnp.concatenate([ref[c, xx].reshape(SHARD, ROWS) for c in range(2)], axis=0)
        lrow[h, :, pl.ds(xx * 2 * SHARD, 2 * SHARD)] = piece.T

    for p in range(2):
        project(p)
        sum_step(0, p)
    for k in range(1, 4):

        @pl.when(is1)
        def _():
            for xx in range(X):
                if xx == k or (xx, k) == (0, 1):
                    for c in range(2):
                        to_partner(c, xx).start()

        turn(ylo, shards.at[ylo], k - 1)
        for p in range(2):
            sum_step(k, p)
    turn(ylo, shards.at[ylo], 3)

    def own_step(p):
        own = chunk(z, p)
        for way in range(2):
            rs_leaf(way, 3, p).wait_recv()
            own += leaf_in(way, 3, p)[...].astype(jnp.float32)
        for way in (1, 0):
            rs_chain(way, 3 - way, p).wait_recv()
            own += chain_in(way, 3 - way, p)[...].astype(jnp.float32)
        high, low = split_bf16(own)
        both = dot(jnp.concatenate([high, low], axis=0), whi[...], 1, 0)
        rotated = both[:PART] + both[PART:] + dot(high, wlo[...], 1, 0)
        moved = second_decay * mom[pl.ds(p * PART, PART), :] + (1.0 - second_decay) * rotated * rotated
        new_moments[pl.ds(p * PART, PART), :] = moved
        scaled = (rotated / jnp.sqrt(moved + moment_eps)).astype(jnp.bfloat16)
        back = dot(scaled, whi[...], 1, 1) + dot(scaled, wlo[...], 1, 1)
        gathered[ylo, z, p] = back.astype(jnp.bfloat16)

    def origin(way, o, p):
        return gathered.at[ylo, (z + Z - o) % Z if way == 0 else (z + o) % Z, p]

    def ag_chain(way, k, p, back=0):
        ref = origin(way, 2 * k + back, p)
        return remote(ref, ref, ag_s, ac_r.at[way, k, p], far[way])

    def ag_leaf(way, k, p, back=0):
        ref = origin(way, 2 * k + back, p)
        return remote(ref, ref, ag_s, al_r.at[way, k, p], near[way])

    def forward(way, o, p):
        ref = origin(way, o, p)
        remote(ref, ref, y_s, y_r, partner).start()

    def gather_step(k, p):
        for way in range(2):
            last = 3 - way
            if 0 < k <= last + 1:
                ag_chain(way, k - 1, p, 2).wait_recv()
            if k <= last:
                ag_chain(way, k, p).start()
        for way in range(2):
            if k < 4:
                ag_leaf(way, k, p).start()
        if k == 0:
            forward(0, 0, p)
        else:
            for way in range(2):
                if k <= 4 - way:
                    forward(way, 2 * k, p)
            for way in range(2):
                ag_leaf(way, k - 1, p, 1).wait_recv()
                forward(way, 2 * k - 1, p)

    loads[2].wait()
    for p in range(2):
        own_step(p)
        gather_step(0, p)

    @pl.when(is1)
    def _():
        all_from_partner().wait_recv()
        across_cores().start()

    for k in range(1, 5):
        for p in range(2):
            gather_step(k, p)
        if k == 1:
            pl.when(is0)(across_cores().wait_recv)
        elif k < 4:
            for xx in range(2 * k - 4, 2 * k - 2):
                turn(1 - ylo, other, xx)

    for lo, n in SPANS:
        total[:, pl.ds(lo, n)] = dot(lrow[ylo], gathered[ylo, :, :, :, pl.ds(lo, n)].reshape(HALF, n), 1, 0)
    whole = gathered.at[1 - ylo]
    remote(whole, whole, y_s, y_r, partner).wait_recv()
    for lo, n in SPANS:
        rest = dot(lrow[1 - ylo], gathered[1 - ylo, :, :, :, pl.ds(lo, n)].reshape(HALF, n), 1, 0)
        update[:, pl.ds(lo, n)] = (total[:, pl.ds(lo, n)] + rest).astype(jnp.bfloat16)

    pl.when(at_home)(to_across.wait_send)
    pl.when(away)(to_mate.wait_send)
    pl.when(away)(to_diagonal.wait_send)
    for r in range(2):
        for d in range(1, X):
            to_x(r, d).wait_send()
        to_core(r).wait_send()
    pl.when(is1)(all_from_partner().wait_send)
    pl.when(is1)(across_cores().wait_send)
    remote(rows.at[ylo], rows.at[ylo], g_s, g_r, partner).wait_send()
    remote(slots, slots, rs_s, o_r, partner).wait_send()
    sent = gathered.at[ylo, pl.ds(0, Z - 1)]
    remote(sent, sent, ag_s, o_r, partner).wait_send()
    remote(whole, whole, y_s, y_r, partner).wait_send()


def per_device(grad, left_basis, right_basis, moments):
    bf16, f32 = jnp.bfloat16, jnp.float32
    dma = pltpu.SemaphoreType.DMA
    vmem = pl.BlockSpec(memory_space=pltpu.VMEM)
    hbm = pl.BlockSpec(memory_space=pl.ANY)
    scratch = [
        pltpu.VMEM((2, 2, X, 2, 2, PART, ROWS), bf16),
        pltpu.VMEM((2, X, 2, 2, PART, ROWS), bf16),
        pltpu.VMEM((2, ROWS, HALF), bf16),
        pltpu.VMEM((2, ROWS, COLS), bf16),
        pltpu.VMEM((COLS, COLS), f32),
        pltpu.VMEM((COLS, COLS), bf16),
        pltpu.VMEM((COLS, COLS), bf16),
        pltpu.VMEM((OWN, COLS), f32),
        pltpu.VMEM((2, Z, PART, COLS), f32),
        pltpu.VMEM((9, 2, PART, COLS), bf16),
        pltpu.VMEM((15, 2, PART, COLS), bf16),
        pltpu.VMEM((2, Z, 2, PART, COLS), bf16),
        pltpu.VMEM((ROWS, COLS), f32),
    ]
    scratch += [dma((4,)), dma((2,)), dma((2,)), dma((2, 3)), dma((2, 3)), dma((2,)), dma((2,)), dma, dma, dma, dma, dma, dma]
    scratch += [dma, dma((2, 4, 2)), dma((2, 4, 2)), dma, dma((2, 4, 2)), dma((2, 4, 2)), dma, dma]
    return pl.pallas_call(
        kernel,
        out_shape=(pltpu.VMEM((OWN, COLS), f32), pltpu.VMEM((ROWS, COLS), bf16)),
        in_specs=[hbm, hbm, hbm, hbm],
        out_specs=(vmem, vmem),
        scratch_shapes=scratch,
        compiler_params=pltpu.CompilerParams(
            collective_id=0, has_side_effects=True, vmem_limit_bytes=62 * 2**20
        ),
    )(grad, left_basis.T.reshape(2, 2, PART, ROWS), right_basis, moments)


def solution(mesh):
    return jax.shard_map(
        per_device,
        mesh=mesh,
        in_specs=(P("dp", "tensor"), P("dp", "tensor"), P("tensor", None), P("dp", "tensor")),
        out_specs=(P("dp", "tensor"), P("dp", "tensor")),
        check_vma=False,
    )
```

```python
import jax
import jax.numpy as jnp
from jax import lax
from jax.experimental import pallas as pl
from jax.experimental.pallas import tpu as pltpu
from jax.sharding import PartitionSpec as P

second_decay = 0.95
moment_eps = 1e-08

MESH = pl.DeviceIdType.MESH
Z, X = 16, 4
ROWS, COLS, OWN, SHARD = 256, 896, 32, 64
HALF = Z * OWN
JS = 2 * X
SPANS = ((0, 256), (256, 256), (512, 256), (768, 128))
PART = OWN // 2
GPARTS = len(SPANS)
GFIRST = 2


def split_bf16(values):
    high = values.astype(jnp.bfloat16)
    return high, (values - high.astype(jnp.float32)).astype(jnp.bfloat16)


def dot(a, b, ca, cb):
    return lax.dot_general(a, b, (((ca,), (cb,)), ((), ())), preferred_element_type=jnp.float32)


def kernel(grad, left, right, moments, new_moments, update, *scratch):
    (shards, other, lrow, rows, w32, whi, wlo, mom, proj, leaving, slots, gathered, total, thi) = scratch[:14]
    (loc_s, l_s, l_r, lx_s, lx_r, lc_s, lc_r, g_s, g_r, o_s, o_r, od_s, od_r) = scratch[14:27]
    (rs_s, rc_r, rl_r, ag_s, ac_r, al_r, y_s, y_r, row_ok, yk_r, a2_s, a2_r) = scratch[27:]
    dp, t = lax.axis_index("dp"), lax.axis_index("tensor")
    ylo, z = dp // Z, dp % Z
    yhi, j = t // JS, t % JS
    x, core = j // 2, j % 2
    is0, is1 = core == 0, core == 1

    def along(step):
        return (ylo * Z + (z + Z + step) % Z, t)

    near, far = (along(1), along(-1)), (along(2), along(-2))

    def beside(step):
        return ((1 - ylo) * Z + (z + Z + step) % Z, t)

    partner = ((1 - ylo) * Z + z, t)
    across = (dp, (1 - yhi) * JS + j)
    diagonal = ((1 - ylo) * Z + z, (1 - yhi) * JS + j)
    sibling = (dp, yhi * JS + x * 2 + (1 - core))
    xs = [(dp, yhi * JS + ((x + d) % X) * 2 + core) for d in range(1, X)]

    def remote(src, dst, ssem, rsem, dev):
        return pltpu.make_async_remote_copy(
            src_ref=src, dst_ref=dst, send_sem=ssem, recv_sem=rsem, device_id=dev, device_id_type=MESH
        )

    barrier = pltpu.get_barrier_semaphore()
    everyone = [*near, *far, partner, across, diagonal, sibling] + xs
    for dev in everyone:
        pl.semaphore_signal(barrier, inc=1, device_id=dev, device_id_type=MESH)
    here = shards.at[ylo, core, x]
    loads = [
        pltpu.make_async_copy(grad, rows.at[ylo], loc_s.at[0]),
        pltpu.make_async_copy(right, w32, loc_s.at[1]),
        pltpu.make_async_copy(moments, mom, loc_s.at[2]),
    ]
    keep = pltpu.make_async_copy(left, here, loc_s.at[3])
    at_home = ylo == yhi
    away = jnp.logical_not(at_home)
    pl.when(at_home)(keep.start)
    for load in loads:
        load.start()
    pl.semaphore_wait(barrier, len(everyone))
    pl.semaphore_signal(row_ok, inc=1, device_id=partner, device_id_type=MESH)

    to_across = remote(left, here, l_s.at[0], l_r.at[ylo], across)
    to_mate = remote(left, here, l_s.at[0], l_r.at[ylo], partner)
    to_diagonal = remote(left, here, l_s.at[1], l_r.at[ylo], diagonal)
    pl.when(at_home)(to_across.start)
    pl.when(away)(to_mate.start)
    pl.when(away)(to_diagonal.start)

    def grad_part(p):
        lo, n = SPANS[p]
        cut = rows.at[ylo, :, pl.ds(lo, n)]
        return remote(grad.at[:, pl.ds(lo, n)], cut, g_s, g_r.at[p], partner)

    for p in range(GFIRST):
        grad_part(p).start()

    def to_x(r, d):
        ref = shards.at[r, core, x]
        return remote(ref, ref, lx_s.at[r, d - 1], lx_r.at[r, d - 1], xs[d - 1])

    def from_x(r, d):
        ref = shards.at[r, core, (x + X - d) % X]
        return remote(ref, ref, lx_s.at[r, d - 1], lx_r.at[r, d - 1], xs[d - 1])

    def to_core(r):
        ref = shards.at[r, core]
        return remote(ref, ref, lc_s.at[r], lc_r.at[r], sibling)

    def from_core(r):
        ref = shards.at[r, 1 - core]
        return remote(ref, ref, lc_s.at[r], lc_r.at[r], sibling)

    for k in range(2):
        r = (ylo + k) % 2
        arrived = remote(left, shards.at[r, core, x], l_s.at[0], l_r.at[r], sibling).wait_recv
        if k == 0:
            pl.when(at_home)(keep.wait)
            pl.when(away)(arrived)
        else:
            arrived()
        for d in range(1, X):
            to_x(r, d).start()

    for p in range(GFIRST, GPARTS):
        grad_part(p).start()
    loads[1].wait()
    for lo in range(0, COLS, 128):
        high, low = split_bf16(w32[pl.ds(lo, 128), :])
        whi[pl.ds(lo, 128), :] = high
        wlo[pl.ds(lo, 128), :] = low
        thi[:, pl.ds(lo, 128)] = high.T

    for k in range(2):
        r = (ylo + k) % 2
        for d in range(1, X):
            from_x(r, d).wait_recv()
        to_core(r).start()

    loads[0].wait()
    for r in range(2):
        from_core(r).wait_recv()

    def term(r, p, lo, n):
        part = dot(shards[r, :, :, :, p].reshape(HALF // 2, ROWS), rows[r, :, pl.ds(lo, n)], 1, 0)
        return part.reshape(Z, PART, n)

    for p in range(2):
        for lo, n in SPANS:
            proj[p, :, :, pl.ds(lo, n)] = term(ylo, p, lo, n)

    def project(p):
        for i, (lo, n) in enumerate(SPANS):
            if p == 0:
                grad_part(i).wait_recv()
            proj[p, :, :, pl.ds(lo, n)] += term(1 - ylo, p, lo, n)

    def chunk(d, p):
        d = (d + Z) % Z
        return proj[p, ((d // 2) % 2) * JS + (d // 4) * 2 + d % 2]

    def chain_in(way, k, p):
        return slots.at[4 * way + k, p]

    def leaf_in(way, k, p):
        return slots.at[7 + 4 * way + k, p]

    def chain_source(way, k, p):
        if way == 0:
            return leaving.at[0, p] if k == 0 else chain_in(0, k - 1, p)
        return leaf_in(1, k, p)

    def rs_chain(way, k, p):
        return remote(chain_source(way, k, p), chain_in(way, k, p), rs_s, rc_r.at[way, k, p], far[way])

    def rs_leaf(way, k, p):
        return remote(leaving.at[1 + 4 * way + k, p], leaf_in(way, k, p), rs_s, rl_r.at[way, k, p], near[way])

    def send_leaf(way, k, p):
        leaving[1 + 4 * way + k, p] = chunk(z + 7 - 2 * k if way == 0 else z - 7 + 2 * k, p).astype(jnp.bfloat16)
        rs_leaf(way, k, p).start()

    def send_chain(way, k, p):
        mine = chunk(z + 8 - 2 * k if way == 0 else z - 6 + 2 * k, p)
        leaf = k - 1 if way == 0 else k
        if leaf >= 0:
            rs_leaf(way, leaf, p).wait_recv()
            mine += leaf_in(way, leaf, p)[...].astype(jnp.float32)
        if k > 0:
            rs_chain(way, k - 1, p).wait_recv()
            mine += chain_in(way, k - 1, p)[...].astype(jnp.float32)
        chain_source(way, k, p)[...] = mine.astype(jnp.bfloat16)
        rs_chain(way, k, p).start()

    def sum_step(k, p):
        if k > 0:
            send_chain(1, k - 1, p)
        send_chain(0, k, p)
        if k == 0:
            send_leaf(1, 0, p)
        send_leaf(0, k, p)
        if k < 3:
            send_leaf(1, k + 1, p)

    def to_partner(c, xx):
        return remote(shards.at[1 - ylo, c, xx], other.at[c, xx], o_s, o_r, partner)

    def all_from_partner():
        return remote(other, other, o_s, o_r, partner)

    def across_cores():
        return remote(other, other, od_s, od_r, sibling)

    def turn(h, ref, xx):
        piece = jnp.concatenate([ref[c, xx].reshape(SHARD, ROWS) for c in range(2)], axis=0)
        lrow[h, :, pl.ds(xx * 2 * SHARD, 2 * SHARD)] = piece.T

    for p in range(2):
        project(p)
        sum_step(0, p)
    for k in range(1, 4):

        @pl.when(is1)
        def _():
            for xx in range(X):
                if xx == k or (xx, k) == (0, 1):
                    for c in range(2):
                        to_partner(c, xx).start()

        turn(ylo, shards.at[ylo], k - 1)
        for p in range(2):
            sum_step(k, p)
    turn(ylo, shards.at[ylo], 3)

    def own_step(p):
        own = chunk(z, p)
        for way in range(2):
            rs_leaf(way, 3, p).wait_recv()
            own += leaf_in(way, 3, p)[...].astype(jnp.float32)
        for way in (1, 0):
            rs_chain(way, 3 - way, p).wait_recv()
            own += chain_in(way, 3 - way, p)[...].astype(jnp.float32)
        high, low = split_bf16(own)
        both = dot(jnp.concatenate([high, low], axis=0), whi[...], 1, 0)
        rotated = both[:PART] + both[PART:] + dot(high, wlo[...], 1, 0)
        moved = second_decay * mom[pl.ds(p * PART, PART), :] + (1.0 - second_decay) * rotated * rotated
        new_moments[pl.ds(p * PART, PART), :] = moved
        scaled = (rotated / jnp.sqrt(moved + moment_eps)).astype(jnp.bfloat16)
        gathered[ylo, z, p] = dot(scaled, thi[...], 1, 0).astype(jnp.bfloat16)

    def origin(way, o, p):
        return gathered.at[ylo, (z + Z - o) % Z if way == 0 else (z + o) % Z, p]

    def ag_chain(way, k, p, back=0):
        ref = origin(way, 2 * k + back, p)
        return remote(ref, ref, ag_s, ac_r.at[way, k, p], far[way])

    def ag_leaf(way, k, p, back=0):
        ref = origin(way, 2 * k + back, p)
        return remote(ref, ref, ag_s, al_r.at[way, k, p], near[way])

    def forward(way, o, p, dev=partner, arrives=None):
        ref = origin(way, o, p)
        remote(ref, ref, y_s, y_r if arrives is None else arrives, dev).start()

    def other_from(o, p):
        return gathered.at[1 - ylo, (z + o) % Z, p]

    def pass_other(k, p):
        ref = other_from(2 * k, p)
        remote(ref, ref, y_s, yk_r.at[k, p], partner).wait_recv()
        remote(ref, ref, a2_s, a2_r.at[k, p], near[1]).start()

    def other_passed(k, p):
        ref = other_from(2 * k + 1, p)
        remote(ref, ref, a2_s, a2_r.at[k, p], near[1]).wait_recv()

    def gather_step(k, p):
        for way in range(2):
            last = 3 - way
            if 0 < k <= last + 1:
                ag_chain(way, k - 1, p, 2).wait_recv()
            if k <= last:
                ag_chain(way, k, p).start()
        for way in range(2):
            if k < 4:
                ag_leaf(way, k, p).start()
        if k == 3:
            if p == 0:
                pl.semaphore_wait(row_ok, 1)
            forward(0, 6, p, beside(2))
            forward(0, 6, p, beside(1))
            forward(1, 6, p, beside(-1))
        if k == 0:
            forward(0, 0, p, arrives=yk_r.at[0, p])
        elif k == 4:
            for way in range(2):
                ag_leaf(way, k - 1, p, 1).wait_recv()
        else:
            forward(0, 2 * k, p)
            forward(1, 2 * k, p, arrives=yk_r.at[k, p] if k < 3 else None)
            for way in range(2):
                ag_leaf(way, k - 1, p, 1).wait_recv()
            forward(0, 2 * k - 1, p)
            pass_other(k - 1, p)

    loads[2].wait()
    for p in range(2):
        own_step(p)
        gather_step(0, p)

    @pl.when(is1)
    def _():
        all_from_partner().wait_recv()
        across_cores().start()

    for k in range(1, 5):
        for p in range(2):
            gather_step(k, p)
        if k == 1:
            pl.when(is0)(across_cores().wait_recv)
        elif k < 4:
            for xx in range(2 * k - 4, 2 * k - 2):
                turn(1 - ylo, other, xx)

    for lo, n in SPANS:
        total[:, pl.ds(lo, n)] = dot(lrow[ylo], gathered[ylo, :, :, :, pl.ds(lo, n)].reshape(HALF, n), 1, 0)
    most = gathered.at[1 - ylo, pl.ds(0, 10)]
    remote(most, most, y_s, y_r, partner).wait_recv()
    for k in range(3):
        for p in range(2):
            other_passed(k, p)
    for lo, n in SPANS:
        rest = dot(lrow[1 - ylo], gathered[1 - ylo, :, :, :, pl.ds(lo, n)].reshape(HALF, n), 1, 0)
        update[:, pl.ds(lo, n)] = (total[:, pl.ds(lo, n)] + rest).astype(jnp.bfloat16)

    pl.when(at_home)(to_across.wait_send)
    pl.when(away)(to_mate.wait_send)
    pl.when(away)(to_diagonal.wait_send)
    for r in range(2):
        for d in range(1, X):
            to_x(r, d).wait_send()
        to_core(r).wait_send()
    pl.when(is1)(all_from_partner().wait_send)
    pl.when(is1)(across_cores().wait_send)
    remote(rows.at[ylo], rows.at[ylo], g_s, g_r, partner).wait_send()
    remote(slots, slots, rs_s, o_r, partner).wait_send()
    sent = gathered.at[ylo, pl.ds(0, Z - 1)]
    remote(sent, sent, ag_s, o_r, partner).wait_send()
    sent = gathered.at[1 - ylo, pl.ds(0, 13)]
    remote(sent, sent, y_s, y_r, partner).wait_send()
    sent = gathered.at[1 - ylo, pl.ds(0, 3)]
    remote(sent, sent, a2_s, y_r, partner).wait_send()


def per_device(grad, left_basis, right_basis, moments):
    bf16, f32 = jnp.bfloat16, jnp.float32
    dma = pltpu.SemaphoreType.DMA
    vmem = pl.BlockSpec(memory_space=pltpu.VMEM)
    hbm = pl.BlockSpec(memory_space=pl.ANY)
    scratch = [
        pltpu.VMEM((2, 2, X, 2, 2, PART, ROWS), bf16),
        pltpu.VMEM((2, X, 2, 2, PART, ROWS), bf16),
        pltpu.VMEM((2, ROWS, HALF), bf16),
        pltpu.VMEM((2, ROWS, COLS), bf16),
        pltpu.VMEM((COLS, COLS), f32),
        pltpu.VMEM((COLS, COLS), bf16),
        pltpu.VMEM((COLS, COLS), bf16),
        pltpu.VMEM((OWN, COLS), f32),
        pltpu.VMEM((2, Z, PART, COLS), f32),
        pltpu.VMEM((9, 2, PART, COLS), bf16),
        pltpu.VMEM((15, 2, PART, COLS), bf16),
        pltpu.VMEM((2, Z, 2, PART, COLS), bf16),
        pltpu.VMEM((ROWS, COLS), f32),
        pltpu.VMEM((COLS, COLS), bf16),
    ]
    scratch += [dma((4,)), dma((2,)), dma((2,)), dma((2, 3)), dma((2, 3)), dma((2,)), dma((2,)), dma, dma((GPARTS,)), dma, dma, dma, dma]
    scratch += [dma, dma((2, 4, 2)), dma((2, 4, 2)), dma, dma((2, 4, 2)), dma((2, 4, 2)), dma, dma, pltpu.SemaphoreType.REGULAR]
    scratch += [dma((3, 2)), dma, dma((3, 2))]
    return pl.pallas_call(
        kernel,
        out_shape=(pltpu.VMEM((OWN, COLS), f32), pltpu.VMEM((ROWS, COLS), bf16)),
        in_specs=[hbm, hbm, hbm, hbm],
        out_specs=(vmem, vmem),
        scratch_shapes=scratch,
        compiler_params=pltpu.CompilerParams(
            collective_id=0, has_side_effects=True, vmem_limit_bytes=62 * 2**20
        ),
    )(grad, left_basis.T.reshape(2, 2, PART, ROWS), right_basis, moments)


def solution(mesh):
    return jax.shard_map(
        per_device,
        mesh=mesh,
        in_specs=(P("dp", "tensor"), P("dp", "tensor"), P("tensor", None), P("dp", "tensor")),
        out_specs=(P("dp", "tensor"), P("dp", "tensor")),
        check_vma=False,
    )
```

```python
import jax
import jax.numpy as jnp
from jax import lax
from jax.experimental import pallas as pl
from jax.experimental.pallas import tpu as pltpu
from jax.sharding import PartitionSpec as P

second_decay = 0.95
moment_eps = 1e-08

MESH = pl.DeviceIdType.MESH
Z, X = 16, 4
ROWS, COLS, OWN, SHARD = 256, 896, 32, 64
HALF = Z * OWN
JS = 2 * X
SPANS = ((0, 512), (512, 384))
PART = OWN // 2
GPARTS = len(SPANS)
GFIRST = 1


def split_bf16(values):
    high = values.astype(jnp.bfloat16)
    return high, (values - high.astype(jnp.float32)).astype(jnp.bfloat16)


def dot(a, b, ca, cb):
    return lax.dot_general(a, b, (((ca,), (cb,)), ((), ())), preferred_element_type=jnp.float32)


def kernel(grad, left, right, moments, new_moments, update, *scratch):
    (shards, other, lrow, rows, w32, whi, wlo, mom, proj, leaving, slots, gathered, total, thi) = scratch[:14]
    (loc_s, l_s, l_r, lx_s, lx_r, lc_s, lc_r, g_s, g_r, o_s, o_r, od_s, od_r) = scratch[14:27]
    (rs_s, rc_r, rl_r, ag_s, ac_r, al_r, y_s, y_r, row_ok, yk_r, a2_s, a2_r) = scratch[27:]
    dp, t = lax.axis_index("dp"), lax.axis_index("tensor")
    ylo, z = dp // Z, dp % Z
    yhi, j = t // JS, t % JS
    x, core = j // 2, j % 2
    is0, is1 = core == 0, core == 1

    def along(step):
        return (ylo * Z + (z + Z + step) % Z, t)

    near, far = (along(1), along(-1)), (along(2), along(-2))

    def beside(step):
        return ((1 - ylo) * Z + (z + Z + step) % Z, t)

    partner = ((1 - ylo) * Z + z, t)
    across = (dp, (1 - yhi) * JS + j)
    diagonal = ((1 - ylo) * Z + z, (1 - yhi) * JS + j)
    sibling = (dp, yhi * JS + x * 2 + (1 - core))
    xs = [(dp, yhi * JS + ((x + d) % X) * 2 + core) for d in range(1, X)]

    def remote(src, dst, ssem, rsem, dev):
        return pltpu.make_async_remote_copy(
            src_ref=src, dst_ref=dst, send_sem=ssem, recv_sem=rsem, device_id=dev, device_id_type=MESH
        )

    barrier = pltpu.get_barrier_semaphore()
    everyone = [*near, *far, partner, across, diagonal, sibling] + xs
    for dev in everyone:
        pl.semaphore_signal(barrier, inc=1, device_id=dev, device_id_type=MESH)
    here = shards.at[ylo, core, x]
    loads = [
        pltpu.make_async_copy(grad, rows.at[ylo], loc_s.at[0]),
        pltpu.make_async_copy(right, w32, loc_s.at[1]),
        pltpu.make_async_copy(moments, mom, loc_s.at[2]),
    ]
    keep = pltpu.make_async_copy(left, here, loc_s.at[3])
    at_home = ylo == yhi
    away = jnp.logical_not(at_home)
    pl.when(at_home)(keep.start)
    for load in loads:
        load.start()
    pl.semaphore_wait(barrier, len(everyone))
    pl.semaphore_signal(row_ok, inc=1, device_id=partner, device_id_type=MESH)

    to_across = remote(left, here, l_s.at[0], l_r.at[ylo], across)
    to_mate = remote(left, here, l_s.at[0], l_r.at[ylo], partner)
    to_diagonal = remote(left, here, l_s.at[1], l_r.at[ylo], diagonal)
    pl.when(at_home)(to_across.start)
    pl.when(away)(to_mate.start)
    pl.when(away)(to_diagonal.start)

    def grad_part(p):
        lo, n = SPANS[p]
        cut = rows.at[ylo, :, pl.ds(lo, n)]
        return remote(grad.at[:, pl.ds(lo, n)], cut, g_s, g_r.at[p], partner)

    for p in range(GFIRST):
        grad_part(p).start()

    def to_x(r, d):
        ref = shards.at[r, core, x]
        return remote(ref, ref, lx_s.at[r, d - 1], lx_r.at[r, d - 1], xs[d - 1])

    def from_x(r, d):
        ref = shards.at[r, core, (x + X - d) % X]
        return remote(ref, ref, lx_s.at[r, d - 1], lx_r.at[r, d - 1], xs[d - 1])

    def to_core(r):
        ref = shards.at[r, core]
        return remote(ref, ref, lc_s.at[r], lc_r.at[r], sibling)

    def from_core(r):
        ref = shards.at[r, 1 - core]
        return remote(ref, ref, lc_s.at[r], lc_r.at[r], sibling)

    for k in range(2):
        r = (ylo + k) % 2
        arrived = remote(left, shards.at[r, core, x], l_s.at[0], l_r.at[r], sibling).wait_recv
        if k == 0:
            pl.when(at_home)(keep.wait)
            pl.when(away)(arrived)
        else:
            arrived()
        for d in range(1, X):
            to_x(r, d).start()

    for p in range(GFIRST, GPARTS):
        grad_part(p).start()
    loads[1].wait()
    for lo in range(0, COLS, 128):
        high, low = split_bf16(w32[pl.ds(lo, 128), :])
        whi[pl.ds(lo, 128), :] = high
        wlo[pl.ds(lo, 128), :] = low
        thi[:, pl.ds(lo, 128)] = high.T

    for k in range(2):
        r = (ylo + k) % 2
        for d in range(1, X):
            from_x(r, d).wait_recv()
        to_core(r).start()

    loads[0].wait()
    for r in range(2):
        from_core(r).wait_recv()

    def term(r, p, lo, n):
        part = dot(shards[r, :, :, :, p].reshape(HALF // 2, ROWS), rows[r, :, pl.ds(lo, n)], 1, 0)
        return part.reshape(Z, PART, n)

    for p in range(2):
        for lo, n in SPANS:
            proj[p, :, :, pl.ds(lo, n)] = term(ylo, p, lo, n)

    def project(p):
        for i, (lo, n) in enumerate(SPANS):
            if p == 0:
                grad_part(i).wait_recv()
            proj[p, :, :, pl.ds(lo, n)] += term(1 - ylo, p, lo, n)

    def chunk(d, p):
        d = (d + Z) % Z
        return proj[p, ((d // 2) % 2) * JS + (d // 4) * 2 + d % 2]

    def chain_in(way, k, p):
        return slots.at[4 * way + k, p]

    def leaf_in(way, k, p):
        return slots.at[7 + 4 * way + k, p]

    def chain_source(way, k, p):
        if way == 0:
            return leaving.at[0, p] if k == 0 else chain_in(0, k - 1, p)
        return leaf_in(1, k, p)

    def rs_chain(way, k, p):
        return remote(chain_source(way, k, p), chain_in(way, k, p), rs_s, rc_r.at[way, k, p], far[way])

    def rs_leaf(way, k, p):
        return remote(leaving.at[1 + 4 * way + k, p], leaf_in(way, k, p), rs_s, rl_r.at[way, k, p], near[way])

    def send_leaf(way, k, p):
        leaving[1 + 4 * way + k, p] = chunk(z + 7 - 2 * k if way == 0 else z - 7 + 2 * k, p).astype(jnp.bfloat16)
        rs_leaf(way, k, p).start()

    def send_chain(way, k, p):
        mine = chunk(z + 8 - 2 * k if way == 0 else z - 6 + 2 * k, p)
        leaf = k - 1 if way == 0 else k
        if leaf >= 0:
            rs_leaf(way, leaf, p).wait_recv()
            mine += leaf_in(way, leaf, p)[...].astype(jnp.float32)
        if k > 0:
            rs_chain(way, k - 1, p).wait_recv()
            mine += chain_in(way, k - 1, p)[...].astype(jnp.float32)
        chain_source(way, k, p)[...] = mine.astype(jnp.bfloat16)
        rs_chain(way, k, p).start()

    def sum_step(k, p):
        if k > 0:
            send_chain(1, k - 1, p)
        send_chain(0, k, p)
        if k == 0:
            send_leaf(1, 0, p)
        send_leaf(0, k, p)
        if k < 3:
            send_leaf(1, k + 1, p)

    def to_partner(c, xx):
        return remote(shards.at[1 - ylo, c, xx], other.at[c, xx], o_s, o_r, partner)

    def all_from_partner():
        return remote(other, other, o_s, o_r, partner)

    def across_cores():
        return remote(other, other, od_s, od_r, sibling)

    def turn(h, ref, xx):
        piece = jnp.concatenate([ref[c, xx].reshape(SHARD, ROWS) for c in range(2)], axis=0)
        lrow[h, :, pl.ds(xx * 2 * SHARD, 2 * SHARD)] = piece.T

    for p in range(2):
        project(p)
        sum_step(0, p)
    for k in range(1, 4):
        for p in range(2):
            sum_step(k, p)

        @pl.when(is1)
        def _():
            for xx in range(X):
                if xx == k or (xx, k) == (0, 1):
                    for c in range(2):
                        to_partner(c, xx).start()

        turn(ylo, shards.at[ylo], k - 1)
    turn(ylo, shards.at[ylo], 3)

    def own_step(p):
        own = chunk(z, p)
        for way in range(2):
            rs_leaf(way, 3, p).wait_recv()
            own += leaf_in(way, 3, p)[...].astype(jnp.float32)
        for way in (1, 0):
            rs_chain(way, 3 - way, p).wait_recv()
            own += chain_in(way, 3 - way, p)[...].astype(jnp.float32)
        high, low = split_bf16(own)
        both = dot(jnp.concatenate([high, low], axis=0), whi[...], 1, 0)
        rotated = both[:PART] + both[PART:] + dot(high, wlo[...], 1, 0)
        moved = second_decay * mom[pl.ds(p * PART, PART), :] + (1.0 - second_decay) * rotated * rotated
        new_moments[pl.ds(p * PART, PART), :] = moved
        scaled = (rotated / jnp.sqrt(moved + moment_eps)).astype(jnp.bfloat16)
        gathered[ylo, z, p] = dot(scaled, thi[...], 1, 0).astype(jnp.bfloat16)

    def origin(way, o, p):
        return gathered.at[ylo, (z + Z - o) % Z if way == 0 else (z + o) % Z, p]

    def ag_chain(way, k, p, back=0):
        ref = origin(way, 2 * k + back, p)
        return remote(ref, ref, ag_s, ac_r.at[way, k, p], far[way])

    def ag_leaf(way, k, p, back=0):
        ref = origin(way, 2 * k + back, p)
        return remote(ref, ref, ag_s, al_r.at[way, k, p], near[way])

    def forward(way, o, p, dev=partner, arrives=None):
        ref = origin(way, o, p)
        remote(ref, ref, y_s, y_r if arrives is None else arrives, dev).start()

    def other_from(o, p):
        return gathered.at[1 - ylo, (z + o) % Z, p]

    def pass_other(k, p):
        ref = other_from(2 * k, p)
        remote(ref, ref, y_s, yk_r.at[k, p], partner).wait_recv()
        remote(ref, ref, a2_s, a2_r.at[k, p], near[1]).start()

    def other_passed(k, p):
        ref = other_from(2 * k + 1, p)
        remote(ref, ref, a2_s, a2_r.at[k, p], near[1]).wait_recv()

    def gather_step(k, p):
        for way in range(2):
            last = 3 - way
            if 0 < k <= last + 1:
                ag_chain(way, k - 1, p, 2).wait_recv()
            if k <= last:
                ag_chain(way, k, p).start()
        for way in range(2):
            if k < 4:
                ag_leaf(way, k, p).start()
        if k == 3:
            if p == 0:
                pl.semaphore_wait(row_ok, 1)
            forward(0, 6, p, beside(2))
            forward(0, 6, p, beside(1))
            forward(1, 6, p, beside(-1))
        if k == 0:
            forward(0, 0, p, arrives=yk_r.at[0, p])
        elif k == 4:
            for way in range(2):
                ag_leaf(way, k - 1, p, 1).wait_recv()
        else:
            forward(0, 2 * k, p)
            forward(1, 2 * k, p, arrives=yk_r.at[k, p] if k < 3 else None)
            for way in range(2):
                ag_leaf(way, k - 1, p, 1).wait_recv()
            forward(0, 2 * k - 1, p)
            pass_other(k - 1, p)

    loads[2].wait()
    for p in range(2):
        own_step(p)
        gather_step(0, p)

    @pl.when(is1)
    def _():
        all_from_partner().wait_recv()
        across_cores().start()

    for k in range(1, 5):
        for p in range(2):
            gather_step(k, p)
        if k == 1:
            pl.when(is0)(across_cores().wait_recv)
        elif k < 4:
            for xx in range(2 * k - 4, 2 * k - 2):
                turn(1 - ylo, other, xx)

    for lo, n in SPANS:
        total[:, pl.ds(lo, n)] = dot(lrow[ylo], gathered[ylo, :, :, :, pl.ds(lo, n)].reshape(HALF, n), 1, 0)
    most = gathered.at[1 - ylo, pl.ds(0, 10)]
    remote(most, most, y_s, y_r, partner).wait_recv()
    for k in range(3):
        for p in range(2):
            other_passed(k, p)
    for lo, n in SPANS:
        rest = dot(lrow[1 - ylo], gathered[1 - ylo, :, :, :, pl.ds(lo, n)].reshape(HALF, n), 1, 0)
        update[:, pl.ds(lo, n)] = (total[:, pl.ds(lo, n)] + rest).astype(jnp.bfloat16)

    pl.when(at_home)(to_across.wait_send)
    pl.when(away)(to_mate.wait_send)
    pl.when(away)(to_diagonal.wait_send)
    for r in range(2):
        for d in range(1, X):
            to_x(r, d).wait_send()
        to_core(r).wait_send()
    pl.when(is1)(all_from_partner().wait_send)
    pl.when(is1)(across_cores().wait_send)
    remote(rows.at[ylo], rows.at[ylo], g_s, g_r, partner).wait_send()
    remote(slots, slots, rs_s, o_r, partner).wait_send()
    sent = gathered.at[ylo, pl.ds(0, Z - 1)]
    remote(sent, sent, ag_s, o_r, partner).wait_send()
    sent = gathered.at[1 - ylo, pl.ds(0, 13)]
    remote(sent, sent, y_s, y_r, partner).wait_send()
    sent = gathered.at[1 - ylo, pl.ds(0, 3)]
    remote(sent, sent, a2_s, y_r, partner).wait_send()


def per_device(grad, left_basis, right_basis, moments):
    bf16, f32 = jnp.bfloat16, jnp.float32
    dma = pltpu.SemaphoreType.DMA
    vmem = pl.BlockSpec(memory_space=pltpu.VMEM)
    hbm = pl.BlockSpec(memory_space=pl.ANY)
    scratch = [
        pltpu.VMEM((2, 2, X, 2, 2, PART, ROWS), bf16),
        pltpu.VMEM((2, X, 2, 2, PART, ROWS), bf16),
        pltpu.VMEM((2, ROWS, HALF), bf16),
        pltpu.VMEM((2, ROWS, COLS), bf16),
        pltpu.VMEM((COLS, COLS), f32),
        pltpu.VMEM((COLS, COLS), bf16),
        pltpu.VMEM((COLS, COLS), bf16),
        pltpu.VMEM((OWN, COLS), f32),
        pltpu.VMEM((2, Z, PART, COLS), f32),
        pltpu.VMEM((9, 2, PART, COLS), bf16),
        pltpu.VMEM((15, 2, PART, COLS), bf16),
        pltpu.VMEM((2, Z, 2, PART, COLS), bf16),
        pltpu.VMEM((ROWS, COLS), f32),
        pltpu.VMEM((COLS, COLS), bf16),
    ]
    scratch += [dma((4,)), dma((2,)), dma((2,)), dma((2, 3)), dma((2, 3)), dma((2,)), dma((2,)), dma, dma((GPARTS,)), dma, dma, dma, dma]
    scratch += [dma, dma((2, 4, 2)), dma((2, 4, 2)), dma, dma((2, 4, 2)), dma((2, 4, 2)), dma, dma, pltpu.SemaphoreType.REGULAR]
    scratch += [dma((3, 2)), dma, dma((3, 2))]
    return pl.pallas_call(
        kernel,
        out_shape=(pltpu.VMEM((OWN, COLS), f32), pltpu.VMEM((ROWS, COLS), bf16)),
        in_specs=[hbm, hbm, hbm, hbm],
        out_specs=(vmem, vmem),
        scratch_shapes=scratch,
        compiler_params=pltpu.CompilerParams(
            collective_id=0, has_side_effects=True, vmem_limit_bytes=62 * 2**20
        ),
    )(grad, left_basis.T.reshape(2, 2, PART, ROWS), right_basis, moments)


def solution(mesh):
    return jax.shard_map(
        per_device,
        mesh=mesh,
        in_specs=(P("dp", "tensor"), P("dp", "tensor"), P("tensor", None), P("dp", "tensor")),
        out_specs=(P("dp", "tensor"), P("dp", "tensor")),
        check_vma=False,
    )
```

```python
import jax
import jax.numpy as jnp
from jax import lax
from jax.experimental import pallas as pl
from jax.experimental.pallas import tpu as pltpu
from jax.sharding import PartitionSpec as P

second_decay = 0.95
moment_eps = 1e-08

MESH = pl.DeviceIdType.MESH
Z, X = 16, 4
ROWS, COLS, OWN, SHARD = 256, 896, 32, 64
HALF = Z * OWN
JS = 2 * X
SPANS = ((0, 512), (512, 384))
PART = OWN // 2
GPARTS = len(SPANS)
GFIRST = 1


def split_bf16(values):
    high = values.astype(jnp.bfloat16)
    return high, (values - high.astype(jnp.float32)).astype(jnp.bfloat16)


def dot(a, b, ca, cb):
    return lax.dot_general(a, b, (((ca,), (cb,)), ((), ())), preferred_element_type=jnp.float32)


def kernel(grad, left, right, moments, new_moments, update, *scratch):
    (shards, other, lrow, rows, w32, whi, wlo, mom, proj, leaving, slots, gathered, total, thi) = scratch[:14]
    (loc_s, l_s, l_r, lx_s, lx_r, lc_s, lc_r, g_s, g_r, o_s, o_r, od_s, od_r) = scratch[14:27]
    (rs_s, rc_r, rl_r, ag_s, ac_r, al_r, y_s, y_r, row_ok, yk_r, a2_s, a2_r) = scratch[27:]
    dp, t = lax.axis_index("dp"), lax.axis_index("tensor")
    ylo, z = dp // Z, dp % Z
    yhi, j = t // JS, t % JS
    x, core = j // 2, j % 2
    is0, is1 = core == 0, core == 1

    def along(step):
        return (ylo * Z + (z + Z + step) % Z, t)

    near, far = (along(1), along(-1)), (along(2), along(-2))

    def beside(step):
        return ((1 - ylo) * Z + (z + Z + step) % Z, t)

    partner = ((1 - ylo) * Z + z, t)
    across = (dp, (1 - yhi) * JS + j)
    diagonal = ((1 - ylo) * Z + z, (1 - yhi) * JS + j)
    sibling = (dp, yhi * JS + x * 2 + (1 - core))
    xs = [(dp, yhi * JS + ((x + d) % X) * 2 + core) for d in range(1, X)]

    def remote(src, dst, ssem, rsem, dev):
        return pltpu.make_async_remote_copy(
            src_ref=src, dst_ref=dst, send_sem=ssem, recv_sem=rsem, device_id=dev, device_id_type=MESH
        )

    barrier = pltpu.get_barrier_semaphore()
    everyone = [*near, *far, partner, across, diagonal, sibling] + xs
    for dev in everyone:
        pl.semaphore_signal(barrier, inc=1, device_id=dev, device_id_type=MESH)
    here = shards.at[ylo, core, x]
    loads = [
        pltpu.make_async_copy(grad, rows.at[ylo], loc_s.at[0]),
        pltpu.make_async_copy(right, w32, loc_s.at[1]),
        pltpu.make_async_copy(moments, mom, loc_s.at[2]),
    ]
    keep = pltpu.make_async_copy(left, here, loc_s.at[3])
    at_home = ylo == yhi
    away = jnp.logical_not(at_home)
    pl.when(at_home)(keep.start)
    for load in loads:
        load.start()
    pl.semaphore_wait(barrier, len(everyone))
    pl.semaphore_signal(row_ok, inc=1, device_id=partner, device_id_type=MESH)

    to_across = remote(left, here, l_s.at[0], l_r.at[ylo], across)
    to_mate = remote(left, here, l_s.at[0], l_r.at[ylo], partner)
    to_diagonal = remote(left, here, l_s.at[1], l_r.at[ylo], diagonal)
    pl.when(at_home)(to_across.start)
    pl.when(away)(to_mate.start)
    pl.when(away)(to_diagonal.start)

    def grad_part(p):
        lo, n = SPANS[p]
        cut = rows.at[ylo, :, pl.ds(lo, n)]
        return remote(grad.at[:, pl.ds(lo, n)], cut, g_s, g_r.at[p], partner)

    for p in range(GFIRST):
        grad_part(p).start()

    def to_x(r, d):
        ref = shards.at[r, core, x]
        return remote(ref, ref, lx_s.at[r, d - 1], lx_r.at[r, d - 1], xs[d - 1])

    def from_x(r, d):
        ref = shards.at[r, core, (x + X - d) % X]
        return remote(ref, ref, lx_s.at[r, d - 1], lx_r.at[r, d - 1], xs[d - 1])

    def to_core(r):
        ref = shards.at[r, core]
        return remote(ref, ref, lc_s.at[r], lc_r.at[r], sibling)

    def from_core(r):
        ref = shards.at[r, 1 - core]
        return remote(ref, ref, lc_s.at[r], lc_r.at[r], sibling)

    for k in range(2):
        r = (ylo + k) % 2
        arrived = remote(left, shards.at[r, core, x], l_s.at[0], l_r.at[r], sibling).wait_recv
        if k == 0:
            pl.when(at_home)(keep.wait)
            pl.when(away)(arrived)
        else:
            arrived()
        for d in range(1, X):
            to_x(r, d).start()

    for p in range(GFIRST, GPARTS):
        grad_part(p).start()
    loads[1].wait()
    for lo in range(0, COLS, 128):
        high, low = split_bf16(w32[pl.ds(lo, 128), :])
        whi[pl.ds(lo, 128), :] = high
        wlo[pl.ds(lo, 128), :] = low
        thi[:, pl.ds(lo, 128)] = high.T

    for k in range(2):
        r = (ylo + k) % 2
        for d in range(1, X):
            from_x(r, d).wait_recv()
        to_core(r).start()

    loads[0].wait()
    for r in range(2):
        from_core(r).wait_recv()

    def term(r, p, lo, n):
        part = dot(shards[r, :, :, :, p].reshape(HALF // 2, ROWS), rows[r, :, pl.ds(lo, n)], 1, 0)
        return part.reshape(Z, PART, n)

    for p in range(2):
        for lo, n in SPANS:
            proj[p, :, :, pl.ds(lo, n)] = term(ylo, p, lo, n)

    def project(p):
        for i, (lo, n) in enumerate(SPANS):
            if p == 0:
                grad_part(i).wait_recv()
            proj[p, :, :, pl.ds(lo, n)] += term(1 - ylo, p, lo, n)

    def chunk(d, p):
        d = (d + Z) % Z
        return proj[p, ((d // 2) % 2) * JS + (d // 4) * 2 + d % 2]

    def chain_in(way, k, p):
        return slots.at[4 * way + k, p]

    def leaf_in(way, k, p):
        return slots.at[7 + 4 * way + k, p]

    def chain_source(way, k, p):
        if way == 0:
            return leaving.at[0, p] if k == 0 else chain_in(0, k - 1, p)
        return leaf_in(1, k, p)

    def rs_chain(way, k, p):
        return remote(chain_source(way, k, p), chain_in(way, k, p), rs_s, rc_r.at[way, k, p], far[way])

    def rs_leaf(way, k, p):
        return remote(leaving.at[1 + 4 * way + k, p], leaf_in(way, k, p), rs_s, rl_r.at[way, k, p], near[way])

    def send_leaf(way, k, p):
        leaving[1 + 4 * way + k, p] = chunk(z + 7 - 2 * k if way == 0 else z - 7 + 2 * k, p).astype(jnp.bfloat16)
        rs_leaf(way, k, p).start()

    def send_chain(way, k, p):
        mine = chunk(z + 8 - 2 * k if way == 0 else z - 6 + 2 * k, p)
        leaf = k - 1 if way == 0 else k
        if leaf >= 0:
            rs_leaf(way, leaf, p).wait_recv()
            mine += leaf_in(way, leaf, p)[...].astype(jnp.float32)
        if k > 0:
            rs_chain(way, k - 1, p).wait_recv()
            mine += chain_in(way, k - 1, p)[...].astype(jnp.float32)
        chain_source(way, k, p)[...] = mine.astype(jnp.bfloat16)
        rs_chain(way, k, p).start()

    def sum_step(k, p):
        if k > 0:
            send_chain(1, k - 1, p)
        send_chain(0, k, p)
        if k == 0:
            send_leaf(1, 0, p)
        send_leaf(0, k, p)
        if k < 3:
            send_leaf(1, k + 1, p)

    def to_partner(c, xx):
        return remote(shards.at[1 - ylo, c, xx], other.at[c, xx], o_s, o_r, partner)

    def all_from_partner():
        return remote(other, other, o_s, o_r, partner)

    def across_cores():
        return remote(other, other, od_s, od_r, sibling)

    def turn(h, ref, xx):
        piece = jnp.concatenate([ref[c, xx].reshape(SHARD, ROWS) for c in range(2)], axis=0)
        lrow[h, :, pl.ds(xx * 2 * SHARD, 2 * SHARD)] = piece.T

    for p in range(2):
        project(p)
        sum_step(0, p)
    for k in range(1, 4):
        for p in range(2):
            sum_step(k, p)

        @pl.when(is1)
        def _():
            for xx in range(X):
                if xx == k or (xx, k) == (0, 1):
                    for c in range(2):
                        to_partner(c, xx).start()

        turn(ylo, shards.at[ylo], k - 1)
    turn(ylo, shards.at[ylo], 3)

    def own_step(p):
        own = chunk(z, p)
        for way in range(2):
            rs_leaf(way, 3, p).wait_recv()
            own += leaf_in(way, 3, p)[...].astype(jnp.float32)
        for way in (1, 0):
            rs_chain(way, 3 - way, p).wait_recv()
            own += chain_in(way, 3 - way, p)[...].astype(jnp.float32)
        high, low = split_bf16(own)
        both = dot(jnp.concatenate([high, low], axis=0), whi[...], 1, 0)
        rotated = both[:PART] + both[PART:] + dot(high, wlo[...], 1, 0)
        moved = second_decay * mom[pl.ds(p * PART, PART), :] + (1.0 - second_decay) * rotated * rotated
        new_moments[pl.ds(p * PART, PART), :] = moved
        scaled = (rotated / jnp.sqrt(moved + moment_eps)).astype(jnp.bfloat16)
        gathered[ylo, z, p] = dot(scaled, thi[...], 1, 0).astype(jnp.bfloat16)

    def origin(way, o, p):
        return gathered.at[ylo, (z + Z - o) % Z if way == 0 else (z + o) % Z, p]

    def ag_chain(way, k, p, back=0):
        ref = origin(way, 2 * k + back, p)
        return remote(ref, ref, ag_s, ac_r.at[way, k, p], far[way])

    def ag_leaf(way, k, p, back=0):
        ref = origin(way, 2 * k + back, p)
        return remote(ref, ref, ag_s, al_r.at[way, k, p], near[way])

    def forward(way, o, p, dev=partner, arrives=None):
        ref = origin(way, o, p)
        remote(ref, ref, y_s, y_r if arrives is None else arrives, dev).start()

    def other_from(o, p):
        return gathered.at[1 - ylo, (z + o) % Z, p]

    def pass_other(k, p):
        ref = other_from(2 * k, p)
        remote(ref, ref, y_s, yk_r.at[k, p], partner).wait_recv()
        remote(ref, ref, a2_s, a2_r.at[k, p], near[1]).start()

    def other_passed(k, p):
        ref = other_from(2 * k + 1, p)
        remote(ref, ref, a2_s, a2_r.at[k, p], near[1]).wait_recv()

    def gather_step(k, p):
        for way in range(2):
            last = 3 - way
            if 0 < k <= last + 1:
                ag_chain(way, k - 1, p, 2).wait_recv()
            if k <= last:
                ag_chain(way, k, p).start()
        if k == 3:
            if p == 0:
                pl.semaphore_wait(row_ok, 1)
            forward(0, 6, p, beside(2))
        for way in range(2):
            if k < 4:
                ag_leaf(way, k, p).start()
        if k == 3:
            forward(0, 6, p, beside(1))
            forward(1, 6, p, beside(-1))
        if k == 0:
            forward(0, 0, p, arrives=yk_r.at[0, p])
        elif k == 4:
            for way in range(2):
                ag_leaf(way, k - 1, p, 1).wait_recv()
        else:
            forward(0, 2 * k, p)
            forward(1, 2 * k, p, arrives=yk_r.at[k, p] if k < 3 else None)
            for way in range(2):
                ag_leaf(way, k - 1, p, 1).wait_recv()
            forward(0, 2 * k - 1, p)
            pass_other(k - 1, p)

    loads[2].wait()
    for p in range(2):
        own_step(p)
        gather_step(0, p)

    @pl.when(is1)
    def _():
        all_from_partner().wait_recv()
        across_cores().start()

    for k in range(1, 5):
        for p in range(2):
            gather_step(k, p)
        if k == 1:
            pl.when(is0)(across_cores().wait_recv)
        elif k < 4:
            for xx in range(2 * k - 4, 2 * k - 2):
                turn(1 - ylo, other, xx)

    for lo, n in SPANS:
        total[:, pl.ds(lo, n)] = dot(lrow[ylo], gathered[ylo, :, :, :, pl.ds(lo, n)].reshape(HALF, n), 1, 0)
    most = gathered.at[1 - ylo, pl.ds(0, 10)]
    remote(most, most, y_s, y_r, partner).wait_recv()
    for k in range(3):
        for p in range(2):
            other_passed(k, p)
    for lo, n in SPANS:
        rest = dot(lrow[1 - ylo], gathered[1 - ylo, :, :, :, pl.ds(lo, n)].reshape(HALF, n), 1, 0)
        update[:, pl.ds(lo, n)] = (total[:, pl.ds(lo, n)] + rest).astype(jnp.bfloat16)

    pl.when(at_home)(to_across.wait_send)
    pl.when(away)(to_mate.wait_send)
    pl.when(away)(to_diagonal.wait_send)
    for r in range(2):
        for d in range(1, X):
            to_x(r, d).wait_send()
        to_core(r).wait_send()
    pl.when(is1)(all_from_partner().wait_send)
    pl.when(is1)(across_cores().wait_send)
    remote(rows.at[ylo], rows.at[ylo], g_s, g_r, partner).wait_send()
    remote(slots, slots, rs_s, o_r, partner).wait_send()
    sent = gathered.at[ylo, pl.ds(0, Z - 1)]
    remote(sent, sent, ag_s, o_r, partner).wait_send()
    sent = gathered.at[1 - ylo, pl.ds(0, 13)]
    remote(sent, sent, y_s, y_r, partner).wait_send()
    sent = gathered.at[1 - ylo, pl.ds(0, 3)]
    remote(sent, sent, a2_s, y_r, partner).wait_send()


def per_device(grad, left_basis, right_basis, moments):
    bf16, f32 = jnp.bfloat16, jnp.float32
    dma = pltpu.SemaphoreType.DMA
    vmem = pl.BlockSpec(memory_space=pltpu.VMEM)
    hbm = pl.BlockSpec(memory_space=pl.ANY)
    scratch = [
        pltpu.VMEM((2, 2, X, 2, 2, PART, ROWS), bf16),
        pltpu.VMEM((2, X, 2, 2, PART, ROWS), bf16),
        pltpu.VMEM((2, ROWS, HALF), bf16),
        pltpu.VMEM((2, ROWS, COLS), bf16),
        pltpu.VMEM((COLS, COLS), f32),
        pltpu.VMEM((COLS, COLS), bf16),
        pltpu.VMEM((COLS, COLS), bf16),
        pltpu.VMEM((OWN, COLS), f32),
        pltpu.VMEM((2, Z, PART, COLS), f32),
        pltpu.VMEM((9, 2, PART, COLS), bf16),
        pltpu.VMEM((15, 2, PART, COLS), bf16),
        pltpu.VMEM((2, Z, 2, PART, COLS), bf16),
        pltpu.VMEM((ROWS, COLS), f32),
        pltpu.VMEM((COLS, COLS), bf16),
    ]
    scratch += [dma((4,)), dma((2,)), dma((2,)), dma((2, 3)), dma((2, 3)), dma((2,)), dma((2,)), dma, dma((GPARTS,)), dma, dma, dma, dma]
    scratch += [dma, dma((2, 4, 2)), dma((2, 4, 2)), dma, dma((2, 4, 2)), dma((2, 4, 2)), dma, dma, pltpu.SemaphoreType.REGULAR]
    scratch += [dma((3, 2)), dma, dma((3, 2))]
    return pl.pallas_call(
        kernel,
        out_shape=(pltpu.VMEM((OWN, COLS), f32), pltpu.VMEM((ROWS, COLS), bf16)),
        in_specs=[hbm, hbm, hbm, hbm],
        out_specs=(vmem, vmem),
        scratch_shapes=scratch,
        compiler_params=pltpu.CompilerParams(
            collective_id=0, has_side_effects=True, vmem_limit_bytes=62 * 2**20
        ),
    )(grad, left_basis.T.reshape(2, 2, PART, ROWS), right_basis, moments)


def solution(mesh):
    return jax.shard_map(
        per_device,
        mesh=mesh,
        in_specs=(P("dp", "tensor"), P("dp", "tensor"), P("tensor", None), P("dp", "tensor")),
        out_specs=(P("dp", "tensor"), P("dp", "tensor")),
        check_vma=False,
    )
```
